32 devices in a mesh: blk: 2 (over x), rows: 16 (over z, y, core).
Axes of the slice: x: 2, y: 2, z: 4, core: 2. Of those that a mesh axis runs over, the one named last changes fastest.
Arguments:
- queries: bfloat16 [32, 4, 8192], P('rows', None, 'blk'), may hold values from -36 to 36
- new_entries: bfloat16 [32, 4, 2, 1024], P('rows', None, None, 'blk'), may hold values from -9 to 9
- resident: bfloat16 [1792, 2, 16, 1024], P('rows', None, None, 'blk'), may hold values from -9 to 9
- swap_area: bfloat16 [256, 2, 16, 1024], P('rows', None, None, 'blk'), may hold values from -9 to 9
- swap_dest: int32 [256], P('rows'), may hold values from 0 to 15, as said below
- page_table: int32 [32, 64], P('rows'), may hold values from 0 to 143, as said below
- lengths: int32 [32], P('rows'), may hold values from 256 to 1024, as said below
- norm_gain: bfloat16 [8192], P('blk'), may hold values from 0.099609375 to 1.8984375
- gate_weight: bfloat16 [8192, 28672], P('blk', 'rows'), may hold values from -0.0625 to 0.0625
- up_weight: bfloat16 [8192, 28672], P('blk', 'rows'), may hold values from -0.0625 to 0.0625
- down_weight: bfloat16 [28672, 8192], P('rows', 'blk'), may hold values from -0.03125 to 0.03125
Outputs:
- attended: bfloat16 [32, 4, 8192], P('rows', None, 'blk')
- layer_out: bfloat16 [32, 4, 8192], P('rows', None, 'blk')
The draws below stay inside these ranges and needn't reach their ends.
Inputs may be any that keep to these rules, and one draw needn't show every extreme that they name: `swap_dest`: every owner sends exactly 2 of its pages to each of 8 different owners (possibly itself), and every owner receives exactly 16 pages. `page_table`: the entries of the 2 rows of one owner name each of its 112 resident pages and each of the 16 pages that land there exactly once; an entry at or above 112 is 112 + s * 2 + k for the k-th page, in the order of the sender's pages, that owner s sends to the row's owner. `lengths`: some row has exactly 1024 cached positions.
All inputs are finite; a program needn't handle non-finite values.
Results may differ from the reference program's by a relative error of at most 0.0086.
Values may be sent and summed in bfloat16 or wider, within the bound.
A program may use at most 128 MiB of HBM per device.

```python
import math
import jax
import jax.numpy as jnp
from jax import lax

KVH = 8
GQ = 8
HD = 128
FF = 28672
PAGE = 16
MAXLEN = 1024
STEPS = 4
CAP = 2
ROWS_DEV = 2
D = 8192
KVD = 1024
MAXPG = 64
OWNERS = 16
SWAP_DEV = 16
RES_DEV = 112
BATCH = 32
N_ROWS = 16


def routing(key):
    base = jax.random.fold_in(key, 11)
    k_sigma, k_tau, k_offset, k_order, k_shuffle = jax.random.split(base, 5)
    sigma = jax.random.permutation(k_sigma, OWNERS)
    tau = jax.random.permutation(k_tau, OWNERS)
    groups = SWAP_DEV // CAP
    offsets = jax.random.permutation(k_offset, OWNERS)[:groups]
    group_dest = sigma[(tau[:, None] + offsets[None, :]) % OWNERS]

    def permute_pages(single):
        return jax.random.permutation(single, SWAP_DEV)
    orders = jax.vmap(permute_pages)(jax.random.split(k_order, OWNERS))
    destination = jnp.take_along_axis(group_dest, orders // CAP, axis=1).astype(jnp.int32)
    target = destination[:, :, None] == jnp.arange(OWNERS, dtype=jnp.int32)[None, None, :]
    before = jnp.cumsum(target.astype(jnp.int32), axis=1) - 1
    ranks = jnp.sum(jnp.where(target, before, 0), axis=2)
    senders = jnp.arange(OWNERS, dtype=jnp.int32)[:, None]
    arrival = destination * (OWNERS * CAP) + senders * CAP + ranks
    ordered = jnp.sort(arrival.reshape(-1)).reshape(OWNERS, SWAP_DEV) % (OWNERS * CAP)
    resident_part = jnp.broadcast_to(jnp.arange(RES_DEV, dtype=jnp.int32)[None, :], (OWNERS, RES_DEV))
    entries = jnp.concatenate([resident_part, RES_DEV + ordered], axis=1)

    def permute_entries(single):
        return jax.random.permutation(single, ROWS_DEV * MAXPG)
    shuffles = jax.vmap(permute_entries)(jax.random.split(k_shuffle, OWNERS))
    entries = jnp.take_along_axis(entries, shuffles, axis=1)
    return (destination.reshape(-1).astype(jnp.int32), entries.reshape(BATCH, MAXPG).astype(jnp.int32))


def draw_swap_dest(key, part):
    return routing(key)[0]


def draw_page_table(key, part):
    return routing(key)[1]


def draw_lengths(key, part):
    drawn = jax.random.randint(jax.random.fold_in(key, 3), (BATCH,), MAXLEN // 4, MAXLEN + 1)
    longest = jax.random.randint(jax.random.fold_in(key, 4), (), 0, BATCH)
    return drawn.at[longest].set(MAXLEN).astype(jnp.int32)


def value_factor():
    rising = 3.0
    head_of = (jnp.arange(KVD) // HD).astype(jnp.float32)
    return 0.5 * rising ** (head_of / (KVH - 1))


def base_values(key, shape):
    return jnp.clip(jax.random.normal(key, shape, jnp.float32), -6.0, 6.0)


def page_values(key, count):
    drawn = base_values(key, (count, 2, PAGE, KVD))
    factors = jnp.stack([jnp.ones((KVD,), jnp.float32), value_factor()])
    return (drawn * factors[None, :, None, :]).astype(jnp.bfloat16)


def draw_resident(key, part):
    return page_values(jax.random.fold_in(key, 5), OWNERS * RES_DEV)


def draw_swap_area(key, part):
    return page_values(jax.random.fold_in(key, 6), OWNERS * SWAP_DEV)


def attention_inputs(key):
    k_query, k_entry = jax.random.split(jax.random.fold_in(key, 23))
    query_draw = base_values(k_query, (BATCH, STEPS, D))
    entry_draw = base_values(k_entry, (BATCH, STEPS, 2, KVD))
    factors = jnp.stack([jnp.ones((KVD,), jnp.float32), value_factor()])
    entry_draw = entry_draw * factors[None, None, :, :]
    return (query_draw.astype(jnp.bfloat16), entry_draw.astype(jnp.bfloat16))


def draw_queries(key, part):
    return attention_inputs(key)[0]


def draw_new_entries(key, part):
    return attention_inputs(key)[1]


def levels(rng, extent, shards, smallest, largest):
    factor_of, own = 1.0, jax.random.fold_in(rng, 6)
    for dim, shards_of in shards:
        heights = jnp.exp(jax.random.uniform(jax.random.fold_in(own, dim), (shards_of,), jnp.float32, smallest / len(shards), largest / len(shards)))
        factor_of = factor_of * jnp.repeat(heights, extent[dim] // shards_of).reshape([-1 if axis == dim else 1 for axis in range(len(extent))])
    return factor_of


def scatter_about(key, shape, width, limit, pieces=(), held_as=jnp.bfloat16):
    values = jax.random.normal(key, shape, jnp.float32) * width
    if len(pieces) > 0:
        values = levels(key, shape, pieces, -0.22, 0.18) * values
    return jnp.clip(values, min=-limit, max=limit).astype(held_as)


def setup_inputs(seed: int = 0) -> dict:
    splits = jax.random.split(jax.random.key(seed), 12)
    return {
        "queries": draw_queries(jax.random.fold_in(splits[11], 71), 0),
        "new_entries": draw_new_entries(jax.random.fold_in(splits[11], 71), 0),
        "resident": draw_resident(jax.random.fold_in(splits[11], 71), 0),
        "swap_area": draw_swap_area(jax.random.fold_in(splits[11], 71), 0),
        "swap_dest": draw_swap_dest(jax.random.fold_in(splits[11], 71), 0),
        "page_table": draw_page_table(jax.random.fold_in(splits[11], 71), 0),
        "lengths": draw_lengths(jax.random.fold_in(splits[11], 71), 0),
        "norm_gain": jnp.clip(1.0 + 0.18 * jax.random.normal(splits[7], (D,), jnp.float32), 0.099609375, 1.8984375).astype(jnp.bfloat16),
        "gate_weight": scatter_about(splits[8], (D, FF), D ** -0.5, 0.0625, ((0, 2), (1, 16))),
        "up_weight": scatter_about(splits[9], (D, FF), D ** -0.5, 0.0625, ((0, 2), (1, 16))),
        "down_weight": scatter_about(splits[10], (FF, D), FF ** -0.5, 0.03125, ((0, 16), (1, 2))),
    }


epsilon = 1e-05

def send_ranks(swap_dest):
    destination = swap_dest.reshape(N_ROWS, SWAP_DEV)
    target = destination[:, :, None] == jnp.arange(N_ROWS, dtype=jnp.int32)[None, None, :]
    before = jnp.cumsum(target.astype(jnp.int32), axis=1) - 1
    return (destination, lax.optimization_barrier(jnp.sum(jnp.where(target, before, 0), axis=2)).astype(jnp.int32))

def reference(queries, new_entries, resident, swap_area, swap_dest, page_table, lengths, norm_gain, gate_weight, up_weight, down_weight):
    destination, ranks = send_ranks(swap_dest)
    senders = jnp.arange(N_ROWS, dtype=jnp.int32)[:, None]
    arrival = (destination * (N_ROWS * CAP) + senders * CAP + ranks).reshape(-1)
    landing = jnp.zeros((N_ROWS * N_ROWS * CAP,), jnp.int32).at[arrival].set(jnp.arange(N_ROWS * SWAP_DEV, dtype=jnp.int32))
    owner = (jnp.arange(BATCH, dtype=jnp.int32) // ROWS_DEV)[:, None]
    resident_ids = owner * RES_DEV + page_table
    slot_ids = owner * (N_ROWS * CAP) + jnp.maximum(page_table - RES_DEV, 0)
    swap_ids = N_ROWS * RES_DEV + landing[slot_ids]
    page_ids = jnp.where(page_table < RES_DEV, resident_ids, swap_ids).astype(jnp.int32)
    page_store = jnp.concatenate([resident, swap_area], axis=0)
    score_scale = 1.0 / math.sqrt(HD)
    causal = jnp.arange(STEPS)[None, :] <= jnp.arange(STEPS)[:, None]

    def one_row(inputs):
        query_row, entry_row, id_row, length = inputs
        fetched = page_store[id_row]
        cached_keys = fetched[:, 0].reshape(MAXLEN, KVH, HD).astype(jnp.float32)
        cached_values = fetched[:, 1].reshape(MAXLEN, KVH, HD).astype(jnp.float32)
        head_queries = query_row.reshape(STEPS, KVH, GQ, HD).astype(jnp.float32)
        new_keys = entry_row[:, 0].reshape(STEPS, KVH, HD).astype(jnp.float32)
        new_values = entry_row[:, 1].reshape(STEPS, KVH, HD).astype(jnp.float32)
        cached_scores = jnp.einsum('skgd,lkd->kgsl', head_queries, cached_keys) * score_scale
        new_scores = jnp.einsum('skgd,tkd->kgst', head_queries, new_keys) * score_scale
        visible = jnp.arange(MAXLEN) < length
        cached_scores = jnp.where(visible[None, None, None, :], cached_scores, -1e+30)
        new_scores = jnp.where(causal[None, None], new_scores, -1e+30)
        row_peak = jnp.maximum(lax.optimization_barrier(jnp.max(cached_scores, axis=-1)), lax.optimization_barrier(jnp.max(new_scores, axis=-1)))[..., None]
        cached_exp = jnp.exp(cached_scores - row_peak)
        new_exp = jnp.exp(new_scores - row_peak)
        row_total = (lax.optimization_barrier(jnp.sum(cached_exp, axis=-1)) + lax.optimization_barrier(jnp.sum(new_exp, axis=-1)))[..., None]
        cached_weights = (cached_exp / row_total).astype(jnp.bfloat16).astype(jnp.float32)
        new_weights = (new_exp / row_total).astype(jnp.bfloat16).astype(jnp.float32)
        mixed_heads = jnp.einsum('kgsl,lkd->skgd', cached_weights, cached_values)
        mixed_heads = mixed_heads + jnp.einsum('kgst,tkd->skgd', new_weights, new_values)
        return mixed_heads.reshape(STEPS, D).astype(jnp.bfloat16)
    attended = lax.map(one_row, (queries, new_entries, page_ids, lengths))
    tokens_flat = attended.reshape(BATCH * STEPS, D)
    tokens_wide = tokens_flat.astype(jnp.float32)
    mean_square = lax.optimization_barrier(jnp.mean(tokens_wide * tokens_wide, axis=1))
    normed = (tokens_wide * norm_gain.astype(jnp.float32)[None, :]).astype(jnp.bfloat16)
    factor = lax.rsqrt(mean_square + epsilon)[:, None]
    gate = factor * jnp.dot(normed, gate_weight, preferred_element_type=jnp.float32)
    up_value = factor * jnp.dot(normed, up_weight, preferred_element_type=jnp.float32)
    hidden = (jax.nn.silu(gate) * up_value).astype(jnp.bfloat16)
    down_sum = jnp.dot(hidden, down_weight, preferred_element_type=jnp.float32)
    layer_out = (tokens_wide + down_sum).astype(jnp.bfloat16).reshape(BATCH, STEPS, D)
    return (attended, layer_out)
```

```python
import functools
import math

import jax
import jax.numpy as jnp
from jax import lax
from jax.experimental import pallas as pl
from jax.experimental.pallas import tpu as pltpu
from jax.sharding import PartitionSpec as P

GQ = 8
HD = 128
PAGE = 16
CAP = 2
TOK = 8
epsilon = 1e-05
MESH = pl.DeviceIdType.MESH
NEG = -1e30


def pack_kernel(dest_ref, swap_ref, out_ref, count_ref, source_ref, sems):
    pages = swap_ref.shape[0]
    slots = out_ref.shape[0]

    @pl.loop(0, slots)
    def _(i):
        source_ref[i] = 0

    @pl.loop(0, slots // CAP)
    def _(i):
        count_ref[i] = 0

    @pl.loop(0, pages)
    def _(i):
        owner = dest_ref[i]
        rank = count_ref[owner]
        count_ref[owner] = rank + 1
        source_ref[owner * CAP + rank] = i

    def copy(i):
        return pltpu.make_async_copy(swap_ref.at[source_ref[i]], out_ref.at[i], sems.at[i])

    @pl.loop(0, slots)
    def _(i):
        copy(i).start()

    @pl.loop(0, slots)
    def _(i):
        copy(i).wait()


def pack_pages(swap_dest, swap_area, owners):
    return pl.pallas_call(
        pack_kernel,
        out_shape=jax.ShapeDtypeStruct((owners * CAP,) + swap_area.shape[1:], swap_area.dtype),
        in_specs=[pl.BlockSpec(memory_space=pltpu.SMEM), pl.BlockSpec(memory_space=pl.ANY)],
        out_specs=pl.BlockSpec(memory_space=pl.ANY),
        scratch_shapes=[
            pltpu.SMEM((owners,), jnp.int32),
            pltpu.SMEM((owners * CAP,), jnp.int32),
            pltpu.SemaphoreType.DMA((owners * CAP,)),
        ],
    )(swap_dest, swap_area)


def layer_kernel(
    cfg,
    q_ref, new_ref, res_bias_ref, swap_bias_ref, gain_ref,
    resident_ref, outgoing_ref, wg_hbm, wu_hbm, wd_hbm,
    att_out, layer_out,
    kv, arrived, wg, wu, wd, att, ag, lhs, gu32, gu16, gu_in, sq_out, sq_in, hid,
    acc, rs, rs_core, rs_y, rs_z,
    kv_sem, w_sem, own_sem,
    sw_s, sw_r, az_s, az_r, ay_s, ay_r, ac_s, ac_r,
    gu_s, gu_r, sq_s, sq_r, hd_s, hd_r,
    rc_s, rc_r, ry_s, ry_r, rz_s, rz_r,
):
    nr, nb, steps, width, parts, fc = cfg
    w2 = width // 2
    zs = nr // 4
    nt, _, tn = ag.shape
    nc = gu32.shape[0]
    kh = width // (GQ * HD)
    rows_here = TOK // steps
    tokens = nr * TOK
    part = tokens // nb
    me = lax.axis_index("rows")
    b = lax.axis_index("blk")
    z, y, c = me // 4, (me // 2) % 2, me % 2

    def row_of(z_, y_, c_):
        return {"rows": z_ * 4 + y_ * 2 + c_}

    kv_copy = pltpu.make_async_copy(resident_ref, kv, kv_sem)
    kv_copy.start()

    def weight_copies(i):
        src, dst = ((wg_hbm, wg), (wu_hbm, wu), (wd_hbm, wd))[i]
        step = dst.shape[0] // parts
        return [
            pltpu.make_async_copy(
                src.at[pl.ds(j * step, step)], dst.at[pl.ds(j * step, step)], w_sem.at[i * parts + j]
            )
            for j in range(parts)
        ]

    barrier = pltpu.get_barrier_semaphore()

    @pl.loop(1, nr)
    def _(k):
        pl.semaphore_signal(
            barrier, inc=1, device_id={"rows": lax.rem(me + k, nr)}, device_id_type=MESH
        )

    for k in range(1, nb):
        pl.semaphore_signal(
            barrier, inc=1, device_id={"blk": lax.rem(b + k, nb)}, device_id_type=MESH
        )
    pl.semaphore_wait(barrier, nr + nb - 2)

    def remote(src, dst, send, recv, device):
        return pltpu.make_async_remote_copy(
            src_ref=src, dst_ref=dst, send_sem=send, recv_sem=recv,
            device_id=device, device_id_type=MESH,
        )

    def swap_copy(k):
        dest = lax.rem(me + k, nr)
        return remote(
            outgoing_ref.at[dest], arrived.at[me], sw_s.at[k], sw_r.at[k], {"rows": dest}
        )

    own_copy = pltpu.make_async_copy(outgoing_ref.at[me], arrived.at[me], own_sem)
    own_copy.start()

    @pl.loop(1, nr)
    def _(k):
        swap_copy(k).start()

    for i in range(3):
        for copy in weight_copies(i):
            copy.start()

    scale = 1.0 / math.sqrt(HD)
    token_row = lax.broadcasted_iota(jnp.int32, (TOK, 1), 0) // steps

    def token_mask(ref):
        mask = jnp.broadcast_to(ref[0:1, :], (TOK, ref.shape[1]))
        for r in range(1, rows_here):
            mask = jnp.where(token_row == r, ref[r : r + 1, :], mask)
        return mask[None] > 0.5

    def scores(qk, keys, mask):
        s = lax.dot_general(
            qk, keys, (((1,), (1,)), ((), ())), preferred_element_type=jnp.float32
        )
        s = (s * scale).reshape(GQ, TOK, s.shape[1])
        return jnp.where(mask, s, NEG)

    def weigh(p, values):
        p2 = p.reshape(GQ * TOK, p.shape[2]).astype(jnp.bfloat16)
        o = jnp.dot(p2, values, preferred_element_type=jnp.float32)
        return o.reshape(GQ, TOK, HD)

    tok_i = lax.broadcasted_iota(jnp.int32, (TOK, new_ref.shape[1]), 0)
    key_i = lax.broadcasted_iota(jnp.int32, (TOK, new_ref.shape[1]), 1)
    new_mask = (
        (tok_i // steps == key_i // steps) & (key_i % steps <= tok_i % steps) & (key_i < TOK)
    )[None]

    q32 = q_ref[...].astype(jnp.float32)
    heads = []
    for k in range(kh):
        heads.append(
            jnp.concatenate(
                [q32[:, (k * GQ + g) * HD : (k * GQ + g + 1) * HD] for g in range(GQ)], axis=0
            ).astype(jnp.bfloat16)
        )
    kv_copy.wait()
    res_mask = token_mask(res_bias_ref)
    n_res = kv.shape[0] * PAGE
    state = []
    for k in range(kh):
        lanes = slice(k * HD, (k + 1) * HD)
        s1 = scores(heads[k], kv[:, 0, :, lanes].reshape(n_res, HD), res_mask)
        s2 = scores(heads[k], new_ref[0, :, lanes], new_mask)
        m = jnp.maximum(jnp.max(s1, axis=-1, keepdims=True), jnp.max(s2, axis=-1, keepdims=True))
        p1, p2 = jnp.exp(s1 - m), jnp.exp(s2 - m)
        l = jnp.sum(p1, axis=-1, keepdims=True) + jnp.sum(p2, axis=-1, keepdims=True)
        o = weigh(p1, kv[:, 1, :, lanes].reshape(n_res, HD)) + weigh(p2, new_ref[1, :, lanes])
        state.append((m, l, o))

    own_copy.wait()

    @pl.loop(1, nr)
    def _(k):
        swap_copy(k).wait_recv()

    swap_mask = token_mask(swap_bias_ref)
    n_swap = nr * CAP * PAGE
    for k in range(kh):
        lanes = slice(k * HD, (k + 1) * HD)
        m1, l1, o1 = state[k]
        s = scores(heads[k], arrived[:, :, 0, :, lanes].reshape(n_swap, HD), swap_mask)
        m = jnp.maximum(m1, jnp.max(s, axis=-1, keepdims=True))
        p = jnp.exp(s - m)
        old = jnp.exp(m1 - m)
        l = l1 * old + jnp.sum(p, axis=-1, keepdims=True)
        o = o1 * old + weigh(p, arrived[:, :, 1, :, lanes].reshape(n_swap, HD))
        o = o / l
        for g in range(GQ):
            att[:, (k * GQ + g) * HD : (k * GQ + g + 1) * HD] = o[g]

    def slots(first, count):
        return pl.ds(pl.multiple_of(first * 16, 16), count * 16)

    column = (c * 2 + y) * zs

    def ag_z(n, k):
        zp = lax.rem(z + k, zs)
        piece = ag.at[n, slots(column + z, 1)]
        return remote(piece, piece, az_s.at[n, k], az_r.at[n, k], row_of(zp, y, c))

    def ag_y(n):
        piece = ag.at[n, slots(column, zs)]
        return remote(piece, piece, ay_s.at[n], ay_r.at[n], row_of(z, 1 - y, c))

    def ag_c(n):
        piece = ag.at[n, slots(c * 2 * zs, 2 * zs)]
        return remote(piece, piece, ac_s.at[n], ac_r.at[n], row_of(z, y, 1 - c))

    for n in range(nt):
        left, right = slice(n * tn, (n + 1) * tn), slice(w2 + n * tn, w2 + (n + 1) * tn)
        ag[n, slots(column + z, 1), :] = jnp.concatenate(
            [att[:, left], att[:, right]], axis=0
        ).astype(jnp.bfloat16)
        for k in range(1, zs):
            ag_z(n, k).start()
    att_out[...] = att[...].astype(jnp.bfloat16)
    for n in range(nt):
        for k in range(1, zs):
            ag_z(n, k).wait_recv()
        ag_y(n).start()
    for n in range(nt):
        ag_y(n).wait_recv()
        ag_c(n).start()
    squares = jnp.zeros((tokens, 1), jnp.float32)
    for n in range(nt):
        ag_c(n).wait_recv()
        wide = ag[n].astype(jnp.float32).reshape(nr, 2, TOK, tn)
        for side in range(2):
            x = wide[:, side].reshape(tokens, tn)
            squares = squares + jnp.sum(x * x, axis=1, keepdims=True)
            lanes = slice(side * w2 + n * tn, side * w2 + (n + 1) * tn)
            lhs[:, lanes] = (x * gain_ref[:, lanes].astype(jnp.float32)).astype(jnp.bfloat16)
    sq_out[...] = jnp.broadcast_to(squares, sq_out.shape)

    def share(p):
        return pl.ds(pl.multiple_of(p * part, 16), part)

    def sq_copy(k):
        p = lax.rem(b + k, nb)
        return remote(
            sq_out.at[share(p)], sq_in.at[k - 1], sq_s.at[k - 1], sq_r.at[k - 1], {"blk": p}
        )

    def gu_copy(j, k):
        p = lax.rem(b + k, nb)
        return remote(
            gu16.at[j, :, share(p)], gu_in.at[j, k - 1],
            gu_s.at[j, k - 1], gu_r.at[j, k - 1], {"blk": p},
        )

    def hid_copy(j, k):
        p = lax.rem(b + k, nb)
        piece = hid.at[j, share(b)]
        return remote(piece, piece, hd_s.at[j, k - 1], hd_r.at[j, k - 1], {"blk": p})

    for k in range(1, nb):
        sq_copy(k).start()
    for copy in weight_copies(0) + weight_copies(1):
        copy.wait()

    def project(j, carry):
        cols = pl.ds(pl.multiple_of(j * fc, fc), fc) if nc > 1 else slice(None)
        for i, w in enumerate((wg, wu)):
            value = jnp.dot(lhs[...], w[:, cols], preferred_element_type=jnp.float32)
            gu32[j, i] = value
            gu16[j, i] = value.astype(jnp.bfloat16)
        for k in range(1, nb):
            gu_copy(j, k).start()
        return carry

    lax.fori_loop(0, nc, project, 0)

    total = sq_out[share(b), 0:1]
    for k in range(1, nb):
        sq_copy(k).wait_recv()
        total = total + sq_in[k - 1, :, 0:1]
    factor = lax.rsqrt(total / (width * nb) + epsilon)

    def activate(j, carry):
        gate = gu32[j, 0, share(b), :]
        up = gu32[j, 1, share(b), :]
        for k in range(1, nb):
            gu_copy(j, k).wait_recv()
            gate = gate + gu_in[j, k - 1, 0].astype(jnp.float32)
            up = up + gu_in[j, k - 1, 1].astype(jnp.float32)
        gate = gate * factor
        up = up * factor
        hid[j, share(b), :] = (gate / (1.0 + jnp.exp(-gate)) * up).astype(jnp.bfloat16)
        for k in range(1, nb):
            hid_copy(j, k).start()
        return carry

    lax.fori_loop(0, nc, activate, 0)
    for copy in weight_copies(2):
        copy.wait()

    @pl.loop(0, nc)
    def _(j):
        for k in range(1, nb):
            hid_copy(j, k).wait_recv()

    def rs_c_copy(n):
        return remote(
            rs.at[n, slots((1 - c) * 2 * zs, 2 * zs)], rs_core.at[n],
            rc_s.at[n], rc_r.at[n], row_of(z, y, 1 - c),
        )

    def rs_y_copy(n):
        return remote(
            rs.at[n, slots((c * 2 + 1 - y) * zs, zs)], rs_y.at[n],
            ry_s.at[n], ry_r.at[n], row_of(z, 1 - y, c),
        )

    def rs_z_copy(n, k):
        zp = lax.rem(z + k, zs)
        return remote(
            rs.at[n, slots(column + zp, 1)], rs_z.at[n, k - 1],
            rz_s.at[n, k - 1], rz_r.at[n, k - 1], row_of(zp, y, c),
        )

    def down(n, carry):
        sides = []
        for side in range(2):
            cols = pl.ds(pl.multiple_of(side * w2 + n * tn, tn), tn)
            value = jnp.zeros((tokens, tn), jnp.float32)
            for j in range(nc):
                value = value + jnp.dot(
                    hid[j], wd[j * fc : (j + 1) * fc, cols], preferred_element_type=jnp.float32
                )
            sides.append(value.reshape(nr, TOK, tn))
        value = jnp.concatenate(sides, axis=1).reshape(nr * 16, tn)
        acc[n] = value
        rs[n] = value.astype(jnp.bfloat16)
        rs_c_copy(n).start()
        return carry

    lax.fori_loop(0, nt, down, 0)

    for n in range(nt):
        rs_c_copy(n).wait_recv()
        mine = slots(c * 2 * zs, 2 * zs)
        value = acc[n, mine, :] + rs_core[n].astype(jnp.float32)
        acc[n, mine, :] = value
        rs[n, mine, :] = value.astype(jnp.bfloat16)
        rs_y_copy(n).start()
    for n in range(nt):
        rs_y_copy(n).wait_recv()
        mine = slots(column, zs)
        value = acc[n, mine, :] + rs_y[n].astype(jnp.float32)
        acc[n, mine, :] = value
        rs[n, mine, :] = value.astype(jnp.bfloat16)
        for k in range(1, zs):
            rs_z_copy(n, k).start()
    for n in range(nt):
        value = acc[n, slots(column + z, 1), :]
        for k in range(1, zs):
            rs_z_copy(n, k).wait_recv()
            value = value + rs_z[n, k - 1].astype(jnp.float32)
        for side in range(2):
            lanes = slice(side * w2 + n * tn, side * w2 + (n + 1) * tn)
            base = att[:, lanes].astype(jnp.bfloat16).astype(jnp.float32)
            att[:, lanes] = base + value[side * TOK : (side + 1) * TOK]
    layer_out[...] = att[...].astype(jnp.bfloat16)

    @pl.loop(1, nr)
    def _(k):
        swap_copy(k).wait_send()

    for k in range(1, nb):
        sq_copy(k).wait_send()

    @pl.loop(0, nc)
    def _(j):
        for k in range(1, nb):
            gu_copy(j, k).wait_send()
            hid_copy(j, k).wait_send()

    for n in range(nt):
        for k in range(1, zs):
            ag_z(n, k).wait_send()
            rs_z_copy(n, k).wait_send()
        ag_y(n).wait_send()
        ag_c(n).wait_send()
        rs_c_copy(n).wait_send()
        rs_y_copy(n).wait_send()


def on_device(
    queries,
    new_entries,
    resident,
    swap_area,
    swap_dest,
    page_table,
    lengths,
    norm_gain,
    gate_weight,
    up_weight,
    down_weight,
):
    nr, nb = lax.axis_size("rows"), lax.axis_size("blk")
    rows_here, steps, width = queries.shape
    kvw = new_entries.shape[-1]
    hidden = gate_weight.shape[1]
    res_pages = resident.shape[0]
    pages_row = page_table.shape[1]
    zs = nr // 4
    w2 = width // 2
    tn = min(512, w2)
    nt = w2 // tn
    fc = 256 if hidden % 256 == 0 else hidden
    nc = hidden // fc
    tokens = nr * TOK
    part = tokens // nb
    parts = 4

    outgoing = pack_pages(swap_dest, swap_area, nr).reshape(nr, CAP, 2, PAGE, kvw)

    total_pages = res_pages + nr * CAP
    place = jnp.arange(total_pages * PAGE, dtype=jnp.int32)
    position = jnp.arange(pages_row, dtype=jnp.int32)[:, None] * PAGE + (place % PAGE)[None, :]
    seen = jnp.any(
        (page_table[:, :, None] == (place // PAGE)[None, None, :])
        & (position[None] < lengths[:, None, None]),
        axis=1,
    ).astype(jnp.float32)
    res_bias = seen[:, : res_pages * PAGE]
    swap_bias = seen[:, res_pages * PAGE :]
    new_kv = jnp.pad(
        new_entries.transpose(2, 0, 1, 3).reshape(2, TOK, kvw), ((0, 0), (0, 128 - TOK), (0, 0))
    )

    bf, f32 = jnp.bfloat16, jnp.float32
    dma = pltpu.SemaphoreType.DMA
    vm = pl.BlockSpec(memory_space=pltpu.VMEM)
    hbm = pl.BlockSpec(memory_space=pl.ANY)
    peers = max(nb - 1, 1)
    zp = max(zs - 1, 1)
    pair = lambda *shape: [dma(shape), dma(shape)]
    attended, layer = pl.pallas_call(
        functools.partial(layer_kernel, (nr, nb, steps, width, parts, fc)),
        out_shape=[jax.ShapeDtypeStruct((TOK, width), bf)] * 2,
        in_specs=[vm] * 5 + [hbm] * 5,
        out_specs=[vm] * 2,
        scratch_shapes=[
            pltpu.VMEM(resident.shape, bf),
            pltpu.VMEM((nr, CAP, 2, PAGE, kvw), bf),
            pltpu.VMEM(gate_weight.shape, bf),
            pltpu.VMEM(up_weight.shape, bf),
            pltpu.VMEM(down_weight.shape, bf),
            pltpu.VMEM((TOK, width), f32),
            pltpu.VMEM((nt, nr * 16, tn), bf),
            pltpu.VMEM((tokens, width), bf),
            pltpu.VMEM((nc, 2, tokens, fc), f32),
            pltpu.VMEM((nc, 2, tokens, fc), bf),
            pltpu.VMEM((nc, peers, 2, part, fc), bf),
            pltpu.VMEM((tokens, 128), f32),
            pltpu.VMEM((peers, part, 128), f32),
            pltpu.VMEM((nc, tokens, fc), bf),
            pltpu.VMEM((nt, nr * 16, tn), f32),
            pltpu.VMEM((nt, nr * 16, tn), bf),
            pltpu.VMEM((nt, 2 * zs * 16, tn), bf),
            pltpu.VMEM((nt, zs * 16, tn), bf),
            pltpu.VMEM((nt, zp, 16, tn), bf),
            dma,
            dma((3 * parts,)),
            dma,
        ]
        + pair(nr) + pair(nt, zs) + pair(nt) + pair(nt)
        + pair(nc, peers) + pair(peers) + pair(nc, peers)
        + pair(nt) + pair(nt) + pair(nt, zp),
        compiler_params=pltpu.CompilerParams(
            collective_id=0, has_side_effects=True, vmem_limit_bytes=62 * 1024 * 1024
        ),
        cost_estimate=pl.CostEstimate(
            flops=6 * tokens * width * hidden,
            bytes_accessed=6 * width * hidden,
            transcendentals=tokens * hidden,
        ),
    )(
        queries.reshape(TOK, width), new_kv, res_bias, swap_bias, norm_gain.reshape(1, width),
        resident, outgoing, gate_weight, up_weight, down_weight,
    )
    shape = (rows_here, steps, width)
    return attended.reshape(shape), layer.reshape(shape)


def solution(mesh):
    placed = (
        P("rows", None, "blk"),
        P("rows", None, None, "blk"),
        P("rows", None, None, "blk"),
        P("rows", None, None, "blk"),
        P("rows"),
        P("rows", None),
        P("rows"),
        P("blk"),
        P("blk", "rows"),
        P("blk", "rows"),
        P("rows", "blk"),
    )
    return jax.shard_map(
        on_device,
        mesh=mesh,
        in_specs=placed,
        out_specs=(P("rows", None, "blk"), P("rows", None, "blk")),
        check_vma=False,
    )
```

```python
import functools
import math

import jax
import jax.numpy as jnp
from jax import lax
from jax.experimental import pallas as pl
from jax.experimental.pallas import tpu as pltpu
from jax.sharding import PartitionSpec as P

GQ = 8
HD = 128
PAGE = 16
CAP = 2
TOK = 8
epsilon = 1e-05
MESH = pl.DeviceIdType.MESH
NEG = -1e30


def layer_kernel(
    cfg,
    source_ref, q_ref, new_ref, seen_ref, gain_ref,
    resident_ref, swap_ref, wg_hbm, wu_hbm, wd_hbm,
    att_out, layer_out,
    kv, swap_in, outgoing, arrived, wg, wu, wd, att, ag, lhs, gu32, gu16, gu_in, sq_out, sq_in, hid,
    acc, rs, rs_core, rs_y, rs_z,
    kv_sem, w_sem, swap_sem,
    sw_s, sw_r, az_s, az_r, ay_s, ay_r, ac_s, ac_r,
    gu_s, gu_r, sq_s, sq_r, hd_s, hd_r,
    rc_s, rc_r, ry_s, ry_r, rz_s, rz_r,
):
    nr, nb, steps, width, parts, fc = cfg
    w2 = width // 2
    zs = nr // 4
    nt, _, tn = ag.shape
    nc = gu32.shape[0]
    kh = width // (GQ * HD)
    rows_here = TOK // steps
    tokens = nr * TOK
    part = tokens // nb
    me = lax.axis_index("rows")
    b = lax.axis_index("blk")
    z, y, c = me // 4, (me // 2) % 2, me % 2

    def row_of(z_, y_, c_):
        return {"rows": z_ * 4 + y_ * 2 + c_}

    swap_load = pltpu.make_async_copy(swap_ref, swap_in, swap_sem)
    swap_load.start()
    kv_copy = pltpu.make_async_copy(resident_ref, kv, kv_sem)
    kv_copy.start()

    def weight_copies(i):
        src, dst = ((wg_hbm, wg), (wu_hbm, wu), (wd_hbm, wd))[i]
        step = dst.shape[0] // parts
        return [
            pltpu.make_async_copy(
                src.at[pl.ds(j * step, step)], dst.at[pl.ds(j * step, step)], w_sem.at[i * parts + j]
            )
            for j in range(parts)
        ]

    barrier = pltpu.get_barrier_semaphore()

    @pl.loop(1, nr)
    def _(k):
        pl.semaphore_signal(
            barrier, inc=1, device_id={"rows": lax.rem(me + k, nr)}, device_id_type=MESH
        )

    for k in range(1, nb):
        pl.semaphore_signal(
            barrier, inc=1, device_id={"blk": lax.rem(b + k, nb)}, device_id_type=MESH
        )
    pl.semaphore_wait(barrier, nr + nb - 2)

    def remote(src, dst, send, recv, device):
        return pltpu.make_async_remote_copy(
            src_ref=src, dst_ref=dst, send_sem=send, recv_sem=recv,
            device_id=device, device_id_type=MESH,
        )

    def swap_copy(k):
        dest = lax.rem(me + k, nr)
        return remote(
            outgoing.at[dest], arrived.at[me], sw_s.at[k], sw_r.at[k], {"rows": dest}
        )

    swap_load.wait()

    @pl.loop(1, nr)
    def _(k):
        dest = lax.rem(me + k, nr)
        for i in range(CAP):
            outgoing[dest, i] = swap_in[source_ref[dest * CAP + i]]
        swap_copy(k).start()

    for i in range(CAP):
        arrived[me, i] = swap_in[source_ref[me * CAP + i]]

    for i in range(3):
        for copy in weight_copies(i):
            copy.start()

    scale = 1.0 / math.sqrt(HD)
    token_row = lax.broadcasted_iota(jnp.int32, (TOK, 1), 0) // steps

    def token_mask(first, count):
        places = slice(first, first + count)
        mask = jnp.broadcast_to(seen_ref[0:1, places], (TOK, count))
        for r in range(1, rows_here):
            mask = jnp.where(token_row == r, seen_ref[r : r + 1, places], mask)
        return mask[None] > 0.5

    def scores(qk, keys, mask):
        s = lax.dot_general(
            qk, keys, (((1,), (1,)), ((), ())), preferred_element_type=jnp.float32
        )
        s = (s * scale).reshape(GQ, TOK, s.shape[1])
        return jnp.where(mask, s, NEG)

    def weigh(p, values):
        p2 = p.reshape(GQ * TOK, p.shape[2]).astype(jnp.bfloat16)
        o = jnp.dot(p2, values, preferred_element_type=jnp.float32)
        return o.reshape(GQ, TOK, HD)

    tok_i = lax.broadcasted_iota(jnp.int32, (TOK, new_ref.shape[1]), 0)
    key_i = lax.broadcasted_iota(jnp.int32, (TOK, new_ref.shape[1]), 1)
    new_mask = (
        (tok_i // steps == key_i // steps) & (key_i % steps <= tok_i % steps) & (key_i < TOK)
    )[None]

    q32 = jnp.concatenate([q_ref[r].astype(jnp.float32) for r in range(rows_here)], axis=0)
    heads = []
    for k in range(kh):
        heads.append(
            jnp.concatenate(
                [q32[:, (k * GQ + g) * HD : (k * GQ + g + 1) * HD] for g in range(GQ)], axis=0
            ).astype(jnp.bfloat16)
        )
    kv_copy.wait()
    n_res = kv.shape[0] * PAGE
    res_mask = token_mask(0, n_res)
    state = []
    for k in range(kh):
        lanes = slice(k * HD, (k + 1) * HD)
        s1 = scores(heads[k], kv[:, 0, :, lanes].reshape(n_res, HD), res_mask)
        s2 = scores(heads[k], new_ref[0, :, lanes], new_mask)
        m = jnp.maximum(jnp.max(s1, axis=-1, keepdims=True), jnp.max(s2, axis=-1, keepdims=True))
        p1, p2 = jnp.exp(s1 - m), jnp.exp(s2 - m)
        l = jnp.sum(p1, axis=-1, keepdims=True) + jnp.sum(p2, axis=-1, keepdims=True)
        o = weigh(p1, kv[:, 1, :, lanes].reshape(n_res, HD)) + weigh(p2, new_ref[1, :, lanes])
        state.append((m, l, o))

    @pl.loop(1, nr)
    def _(k):
        swap_copy(k).wait_recv()

    n_swap = nr * CAP * PAGE
    swap_mask = token_mask(n_res, n_swap)
    for k in range(kh):
        lanes = slice(k * HD, (k + 1) * HD)
        m1, l1, o1 = state[k]
        s = scores(heads[k], arrived[:, :, 0, :, lanes].reshape(n_swap, HD), swap_mask)
        m = jnp.maximum(m1, jnp.max(s, axis=-1, keepdims=True))
        p = jnp.exp(s - m)
        old = jnp.exp(m1 - m)
        l = l1 * old + jnp.sum(p, axis=-1, keepdims=True)
        o = o1 * old + weigh(p, arrived[:, :, 1, :, lanes].reshape(n_swap, HD))
        o = o / l
        for g in range(GQ):
            att[:, (k * GQ + g) * HD : (k * GQ + g + 1) * HD] = o[g]

    def slots(first, count):
        return pl.ds(pl.multiple_of(first * 16, 16), count * 16)

    column = (c * 2 + y) * zs

    def ag_z(n, k):
        zp = lax.rem(z + k, zs)
        piece = ag.at[n, slots(column + z, 1)]
        return remote(piece, piece, az_s.at[n, k], az_r.at[n, k], row_of(zp, y, c))

    def ag_y(n):
        piece = ag.at[n, slots(column, zs)]
        return remote(piece, piece, ay_s.at[n], ay_r.at[n], row_of(z, 1 - y, c))

    def ag_c(n):
        piece = ag.at[n, slots(c * 2 * zs, 2 * zs)]
        return remote(piece, piece, ac_s.at[n], ac_r.at[n], row_of(z, y, 1 - c))

    for n in range(nt):
        left, right = slice(n * tn, (n + 1) * tn), slice(w2 + n * tn, w2 + (n + 1) * tn)
        ag[n, slots(column + z, 1), :] = jnp.concatenate(
            [att[:, left], att[:, right]], axis=0
        ).astype(jnp.bfloat16)
        for k in range(1, zs):
            ag_z(n, k).start()
    for r in range(rows_here):
        att_out[r] = att[r * steps : (r + 1) * steps, :].astype(jnp.bfloat16)
    for n in range(nt):
        for k in range(1, zs):
            ag_z(n, k).wait_recv()
        ag_y(n).start()
    for n in range(nt):
        ag_y(n).wait_recv()
        ag_c(n).start()
    squares = jnp.zeros((tokens, 1), jnp.float32)
    for n in range(nt):
        ag_c(n).wait_recv()
        wide = ag[n].astype(jnp.float32).reshape(nr, 2, TOK, tn)
        for side in range(2):
            x = wide[:, side].reshape(tokens, tn)
            squares = squares + jnp.sum(x * x, axis=1, keepdims=True)
            lanes = slice(side * w2 + n * tn, side * w2 + (n + 1) * tn)
            lhs[:, lanes] = (x * gain_ref[:, lanes].astype(jnp.float32)).astype(jnp.bfloat16)
    sq_out[...] = jnp.broadcast_to(squares, sq_out.shape)

    def share(p):
        return pl.ds(pl.multiple_of(p * part, 16), part)

    def sq_copy(k):
        p = lax.rem(b + k, nb)
        return remote(
            sq_out.at[share(p)], sq_in.at[k - 1], sq_s.at[k - 1], sq_r.at[k - 1], {"blk": p}
        )

    def gu_copy(j, k):
        p = lax.rem(b + k, nb)
        return remote(
            gu16.at[j, :, share(p)], gu_in.at[j, k - 1],
            gu_s.at[j, k - 1], gu_r.at[j, k - 1], {"blk": p},
        )

    def hid_copy(j, k):
        p = lax.rem(b + k, nb)
        piece = hid.at[j, share(b)]
        return remote(piece, piece, hd_s.at[j, k - 1], hd_r.at[j, k - 1], {"blk": p})

    for k in range(1, nb):
        sq_copy(k).start()
    for copy in weight_copies(0) + weight_copies(1):
        copy.wait()

    def project(j, carry):
        cols = pl.ds(pl.multiple_of(j * fc, fc), fc) if nc > 1 else slice(None)
        for i, w in enumerate((wg, wu)):
            value = jnp.dot(lhs[...], w[:, cols], preferred_element_type=jnp.float32)
            gu32[j, i] = value
            gu16[j, i] = value.astype(jnp.bfloat16)
        for k in range(1, nb):
            gu_copy(j, k).start()
        return carry

    lax.fori_loop(0, nc, project, 0)

    total = sq_out[share(b), 0:1]
    for k in range(1, nb):
        sq_copy(k).wait_recv()
        total = total + sq_in[k - 1, :, 0:1]
    factor = lax.rsqrt(total / (width * nb) + epsilon)

    def activate(j, carry):
        gate = gu32[j, 0, share(b), :]
        up = gu32[j, 1, share(b), :]
        for k in range(1, nb):
            gu_copy(j, k).wait_recv()
            gate = gate + gu_in[j, k - 1, 0].astype(jnp.float32)
            up = up + gu_in[j, k - 1, 1].astype(jnp.float32)
        gate = gate * factor
        up = up * factor
        hid[j, share(b), :] = (gate / (1.0 + jnp.exp(-gate)) * up).astype(jnp.bfloat16)
        for k in range(1, nb):
            hid_copy(j, k).start()
        return carry

    lax.fori_loop(0, nc, activate, 0)
    for copy in weight_copies(2):
        copy.wait()

    @pl.loop(0, nc)
    def _(j):
        for k in range(1, nb):
            hid_copy(j, k).wait_recv()

    def rs_c_copy(n):
        return remote(
            rs.at[n, slots((1 - c) * 2 * zs, 2 * zs)], rs_core.at[n],
            rc_s.at[n], rc_r.at[n], row_of(z, y, 1 - c),
        )

    def rs_y_copy(n):
        return remote(
            rs.at[n, slots((c * 2 + 1 - y) * zs, zs)], rs_y.at[n],
            ry_s.at[n], ry_r.at[n], row_of(z, 1 - y, c),
        )

    def rs_z_copy(n, k):
        zp = lax.rem(z + k, zs)
        return remote(
            rs.at[n, slots(column + zp, 1)], rs_z.at[n, k - 1],
            rz_s.at[n, k - 1], rz_r.at[n, k - 1], row_of(zp, y, c),
        )

    def down(n, carry):
        sides = []
        for side in range(2):
            cols = pl.ds(pl.multiple_of(side * w2 + n * tn, tn), tn)
            value = jnp.zeros((tokens, tn), jnp.float32)
            for j in range(nc):
                value = value + jnp.dot(
                    hid[j], wd[j * fc : (j + 1) * fc, cols], preferred_element_type=jnp.float32
                )
            sides.append(value.reshape(nr, TOK, tn))
        value = jnp.concatenate(sides, axis=1).reshape(nr * 16, tn)
        acc[n] = value
        rs[n] = value.astype(jnp.bfloat16)
        rs_c_copy(n).start()
        return carry

    lax.fori_loop(0, nt, down, 0)

    for n in range(nt):
        rs_c_copy(n).wait_recv()
        mine = slots(c * 2 * zs, 2 * zs)
        value = acc[n, mine, :] + rs_core[n].astype(jnp.float32)
        acc[n, mine, :] = value
        rs[n, mine, :] = value.astype(jnp.bfloat16)
        rs_y_copy(n).start()
    for n in range(nt):
        rs_y_copy(n).wait_recv()
        mine = slots(column, zs)
        value = acc[n, mine, :] + rs_y[n].astype(jnp.float32)
        acc[n, mine, :] = value
        rs[n, mine, :] = value.astype(jnp.bfloat16)
        for k in range(1, zs):
            rs_z_copy(n, k).start()
    for n in range(nt):
        value = acc[n, slots(column + z, 1), :]
        for k in range(1, zs):
            rs_z_copy(n, k).wait_recv()
            value = value + rs_z[n, k - 1].astype(jnp.float32)
        for side in range(2):
            lanes = slice(side * w2 + n * tn, side * w2 + (n + 1) * tn)
            base = att[:, lanes].astype(jnp.bfloat16).astype(jnp.float32)
            att[:, lanes] = base + value[side * TOK : (side + 1) * TOK]
    for r in range(rows_here):
        layer_out[r] = att[r * steps : (r + 1) * steps, :].astype(jnp.bfloat16)

    @pl.loop(1, nr)
    def _(k):
        swap_copy(k).wait_send()

    for k in range(1, nb):
        sq_copy(k).wait_send()

    @pl.loop(0, nc)
    def _(j):
        for k in range(1, nb):
            gu_copy(j, k).wait_send()
            hid_copy(j, k).wait_send()

    for n in range(nt):
        for k in range(1, zs):
            ag_z(n, k).wait_send()
            rs_z_copy(n, k).wait_send()
        ag_y(n).wait_send()
        ag_c(n).wait_send()
        rs_c_copy(n).wait_send()
        rs_y_copy(n).wait_send()


def on_device(
    queries,
    new_entries,
    resident,
    swap_area,
    swap_dest,
    page_table,
    lengths,
    norm_gain,
    gate_weight,
    up_weight,
    down_weight,
):
    nr, nb = lax.axis_size("rows"), lax.axis_size("blk")
    rows_here, steps, width = queries.shape
    kvw = new_entries.shape[-1]
    hidden = gate_weight.shape[1]
    res_pages = resident.shape[0]
    pages_row = page_table.shape[1]
    zs = nr // 4
    w2 = width // 2
    tn = min(512, w2)
    nt = w2 // tn
    fc = 256 if hidden % 256 == 0 else hidden
    nc = hidden // fc
    tokens = nr * TOK
    part = tokens // nb
    parts = 4

    index = jnp.arange(swap_dest.shape[0], dtype=jnp.int32)
    same = (swap_dest[:, None] == swap_dest[None, :]) & (index[None, :] < index[:, None])
    slot = swap_dest * CAP + jnp.sum(same.astype(jnp.int32), axis=1)
    goes = slot[None, :] == jnp.arange(nr * CAP, dtype=jnp.int32)[:, None]
    source = jnp.sum(jnp.where(goes, index[None, :], 0), axis=1)

    total_pages = res_pages + nr * CAP
    place = jnp.arange(total_pages * PAGE, dtype=jnp.int32)
    position = jnp.arange(pages_row, dtype=jnp.int32)[:, None] * PAGE + (place % PAGE)[None, :]
    seen = jnp.any(
        (page_table[:, :, None] == (place // PAGE)[None, None, :])
        & (position[None] < lengths[:, None, None]),
        axis=1,
    ).astype(jnp.float32)
    new_kv = jnp.pad(
        new_entries.transpose(2, 0, 1, 3).reshape(2, TOK, kvw), ((0, 0), (0, 128 - TOK), (0, 0))
    )

    bf, f32 = jnp.bfloat16, jnp.float32
    dma = pltpu.SemaphoreType.DMA
    vm = pl.BlockSpec(memory_space=pltpu.VMEM)
    hbm = pl.BlockSpec(memory_space=pl.ANY)
    peers = max(nb - 1, 1)
    zp = max(zs - 1, 1)
    pair = lambda *shape: [dma(shape), dma(shape)]
    attended, layer = pl.pallas_call(
        functools.partial(layer_kernel, (nr, nb, steps, width, parts, fc)),
        out_shape=[jax.ShapeDtypeStruct(queries.shape, bf)] * 2,
        in_specs=[pl.BlockSpec(memory_space=pltpu.SMEM)] + [vm] * 4 + [hbm] * 5,
        out_specs=[vm] * 2,
        scratch_shapes=[
            pltpu.VMEM(resident.shape, bf),
            pltpu.VMEM(swap_area.shape, bf),
            pltpu.VMEM((nr, CAP, 2, PAGE, kvw), bf),
            pltpu.VMEM((nr, CAP, 2, PAGE, kvw), bf),
            pltpu.VMEM(gate_weight.shape, bf),
            pltpu.VMEM(up_weight.shape, bf),
            pltpu.VMEM(down_weight.shape, bf),
            pltpu.VMEM((TOK, width), f32),
            pltpu.VMEM((nt, nr * 16, tn), bf),
            pltpu.VMEM((tokens, width), bf),
            pltpu.VMEM((nc, 2, tokens, fc), f32),
            pltpu.VMEM((nc, 2, tokens, fc), bf),
            pltpu.VMEM((nc, peers, 2, part, fc), bf),
            pltpu.VMEM((tokens, 128), f32),
            pltpu.VMEM((peers, part, 128), f32),
            pltpu.VMEM((nc, tokens, fc), bf),
            pltpu.VMEM((nt, nr * 16, tn), f32),
            pltpu.VMEM((nt, nr * 16, tn), bf),
            pltpu.VMEM((nt, 2 * zs * 16, tn), bf),
            pltpu.VMEM((nt, zs * 16, tn), bf),
            pltpu.VMEM((nt, zp, 16, tn), bf),
            dma,
            dma((3 * parts,)),
            dma,
        ]
        + pair(nr) + pair(nt, zs) + pair(nt) + pair(nt)
        + pair(nc, peers) + pair(peers) + pair(nc, peers)
        + pair(nt) + pair(nt) + pair(nt, zp),
        compiler_params=pltpu.CompilerParams(
            collective_id=0, has_side_effects=True, vmem_limit_bytes=62 * 1024 * 1024
        ),
        cost_estimate=pl.CostEstimate(
            flops=6 * tokens * width * hidden,
            bytes_accessed=6 * width * hidden,
            transcendentals=tokens * hidden,
        ),
    )(
        source, queries, new_kv, seen, norm_gain.reshape(1, width),
        resident, swap_area, gate_weight, up_weight, down_weight,
    )
    return attended, layer


def solution(mesh):
    placed = (
        P("rows", None, "blk"),
        P("rows", None, None, "blk"),
        P("rows", None, None, "blk"),
        P("rows", None, None, "blk"),
        P("rows"),
        P("rows", None),
        P("rows"),
        P("blk"),
        P("blk", "rows"),
        P("blk", "rows"),
        P("rows", "blk"),
    )
    return jax.shard_map(
        on_device,
        mesh=mesh,
        in_specs=placed,
        out_specs=(P("rows", None, "blk"), P("rows", None, "blk")),
        check_vma=False,
    )
```

```python
import functools
import math

import jax
import jax.numpy as jnp
from jax import lax
from jax.experimental import pallas as pl
from jax.experimental.pallas import tpu as pltpu
from jax.sharding import PartitionSpec as P

GQ = 8
HD = 128
PAGE = 16
CAP = 2
TOK = 8
epsilon = 1e-05
MESH = pl.DeviceIdType.MESH
NEG = -1e30


def layer_kernel(
    cfg,
    source_ref, q_ref, new_ref, seen_ref, gain_ref,
    resident_ref, swap_ref, wg_hbm, wu_hbm, wd_hbm,
    att_out, layer_out,
    kv, swap_in, outgoing, arrived, wg, wu, wd, att, ag, lhs, gu32, gu16, gu_in, sq_out, sq_in, hid,
    acc, rs, rs_core, rs_y, rs_z,
    kv_sem, w_sem, swap_sem,
    sw_s, sw_r, az_s, az_r, ay_s, ay_r, ac_s, ac_r,
    gu_s, gu_r, sq_s, sq_r, hd_s, hd_r,
    rc_s, rc_r, ry_s, ry_r, rz_s, rz_r,
):
    nr, nb, steps, width, parts, fc = cfg
    w2 = width // 2
    zs = nr // 4
    nt, _, tn = ag.shape
    nc = gu32.shape[0]
    kh = width // (GQ * HD)
    rows_here = TOK // steps
    tokens = nr * TOK
    part = tokens // nb
    me = lax.axis_index("rows")
    b = lax.axis_index("blk")
    z, y, c = me // 4, (me // 2) % 2, me % 2

    def row_of(z_, y_, c_):
        return {"rows": z_ * 4 + y_ * 2 + c_}

    swap_load = pltpu.make_async_copy(swap_ref, swap_in, swap_sem)
    swap_load.start()
    kv_copy = pltpu.make_async_copy(resident_ref, kv, kv_sem)
    kv_copy.start()

    def weight_copies(i):
        src, dst = ((wg_hbm, wg), (wu_hbm, wu), (wd_hbm, wd))[i]
        step = dst.shape[0] // parts
        return [
            pltpu.make_async_copy(
                src.at[pl.ds(j * step, step)], dst.at[pl.ds(j * step, step)], w_sem.at[i * parts + j]
            )
            for j in range(parts)
        ]

    barrier = pltpu.get_barrier_semaphore()

    @pl.loop(1, nr)
    def _(k):
        pl.semaphore_signal(
            barrier, inc=1, device_id={"rows": lax.rem(me + k, nr)}, device_id_type=MESH
        )

    for k in range(1, nb):
        pl.semaphore_signal(
            barrier, inc=1, device_id={"blk": lax.rem(b + k, nb)}, device_id_type=MESH
        )
    pl.semaphore_wait(barrier, nr + nb - 2)

    def remote(src, dst, send, recv, device):
        return pltpu.make_async_remote_copy(
            src_ref=src, dst_ref=dst, send_sem=send, recv_sem=recv,
            device_id=device, device_id_type=MESH,
        )

    half = nr // 2

    def swap_dest(k):
        return (k // half + 1 + me // half) % 2 * half + (me + k) % half

    def swap_copy(k):
        dest = swap_dest(k)
        return remote(
            outgoing.at[dest], arrived.at[me], sw_s.at[k], sw_r.at[k], {"rows": dest}
        )

    swap_load.wait()

    def swap_send(k):
        dest = swap_dest(k)
        for i in range(CAP):
            outgoing[dest, i] = swap_in[source_ref[dest * CAP + i]]
        swap_copy(k).start()

    pl.loop(0, half)(swap_send)
    pl.loop(half + 1, nr)(swap_send)

    for i in range(CAP):
        arrived[me, i] = swap_in[source_ref[me * CAP + i]]

    for i in range(3):
        for copy in weight_copies(i):
            copy.start()

    acc[...] = jnp.zeros_like(acc)

    scale = 1.0 / math.sqrt(HD)
    token_row = lax.broadcasted_iota(jnp.int32, (TOK, 1), 0) // steps

    def token_mask(first, count):
        places = slice(first, first + count)
        mask = jnp.broadcast_to(seen_ref[0:1, places], (TOK, count))
        for r in range(1, rows_here):
            mask = jnp.where(token_row == r, seen_ref[r : r + 1, places], mask)
        return mask[None] > 0.5

    def scores(qk, keys, mask):
        s = lax.dot_general(
            qk, keys, (((1,), (1,)), ((), ())), preferred_element_type=jnp.float32
        )
        s = (s * scale).reshape(GQ, TOK, s.shape[1])
        return jnp.where(mask, s, NEG)

    def weigh(p, values):
        p2 = p.reshape(GQ * TOK, p.shape[2]).astype(jnp.bfloat16)
        o = jnp.dot(p2, values, preferred_element_type=jnp.float32)
        return o.reshape(GQ, TOK, HD)

    fresh = []
    for i in range(2):
        entries = [new_ref[r].astype(jnp.float32)[:, i, :] for r in range(rows_here)]
        entries.append(jnp.zeros((128 - TOK, new_ref.shape[-1]), jnp.float32))
        fresh.append(jnp.concatenate(entries, axis=0).astype(jnp.bfloat16))
    tok_i = lax.broadcasted_iota(jnp.int32, (TOK, 128), 0)
    key_i = lax.broadcasted_iota(jnp.int32, (TOK, 128), 1)
    new_mask = (
        (tok_i // steps == key_i // steps) & (key_i % steps <= tok_i % steps) & (key_i < TOK)
    )[None]

    q32 = jnp.concatenate([q_ref[r].astype(jnp.float32) for r in range(rows_here)], axis=0)
    heads = []
    for k in range(kh):
        heads.append(
            jnp.concatenate(
                [q32[:, (k * GQ + g) * HD : (k * GQ + g + 1) * HD] for g in range(GQ)], axis=0
            ).astype(jnp.bfloat16)
        )
    kv_copy.wait()
    n_res = kv.shape[0] * PAGE
    res_mask = token_mask(0, n_res)
    state = []
    for k in range(kh):
        lanes = slice(k * HD, (k + 1) * HD)
        s1 = scores(heads[k], kv[:, 0, :, lanes].reshape(n_res, HD), res_mask)
        s2 = scores(heads[k], fresh[0][:, lanes], new_mask)
        m = jnp.maximum(jnp.max(s1, axis=-1, keepdims=True), jnp.max(s2, axis=-1, keepdims=True))
        p1, p2 = jnp.exp(s1 - m), jnp.exp(s2 - m)
        l = jnp.sum(p1, axis=-1, keepdims=True) + jnp.sum(p2, axis=-1, keepdims=True)
        o = weigh(p1, kv[:, 1, :, lanes].reshape(n_res, HD)) + weigh(p2, fresh[1][:, lanes])
        state.append((m, l, o))

    pl.loop(0, half)(lambda k: swap_copy(k).wait_recv())
    pl.loop(half + 1, nr)(lambda k: swap_copy(k).wait_recv())

    n_swap = nr * CAP * PAGE
    swap_mask = token_mask(n_res, n_swap)
    for k in range(kh):
        lanes = slice(k * HD, (k + 1) * HD)
        m1, l1, o1 = state[k]
        s = scores(heads[k], arrived[:, :, 0, :, lanes].reshape(n_swap, HD), swap_mask)
        m = jnp.maximum(m1, jnp.max(s, axis=-1, keepdims=True))
        p = jnp.exp(s - m)
        old = jnp.exp(m1 - m)
        l = l1 * old + jnp.sum(p, axis=-1, keepdims=True)
        o = o1 * old + weigh(p, arrived[:, :, 1, :, lanes].reshape(n_swap, HD))
        o = o / l
        for g in range(GQ):
            att[:, (k * GQ + g) * HD : (k * GQ + g + 1) * HD] = o[g]

    def slots(first, count):
        return pl.ds(pl.multiple_of(first * 16, 16), count * 16)

    column = (c * 2 + y) * zs

    def ag_z(n, k):
        zp = lax.rem(z + k, zs)
        piece = ag.at[n, slots(column + z, 1)]
        return remote(piece, piece, az_s.at[n, k], az_r.at[n, k], row_of(zp, y, c))

    def ag_y(n):
        piece = ag.at[n, slots(column, zs)]
        return remote(piece, piece, ay_s.at[n], ay_r.at[n], row_of(z, 1 - y, c))

    def ag_c(n):
        piece = ag.at[n, slots(c * 2 * zs, 2 * zs)]
        return remote(piece, piece, ac_s.at[n], ac_r.at[n], row_of(z, y, 1 - c))

    for n in range(nt):
        left, right = slice(n * tn, (n + 1) * tn), slice(w2 + n * tn, w2 + (n + 1) * tn)
        ag[n, slots(column + z, 1), :] = jnp.concatenate(
            [att[:, left], att[:, right]], axis=0
        ).astype(jnp.bfloat16)
        for k in range(1, zs):
            ag_z(n, k).start()
    for r in range(rows_here):
        att_out[r] = att[r * steps : (r + 1) * steps, :].astype(jnp.bfloat16)
    for n in range(nt):
        for k in range(1, zs):
            ag_z(n, k).wait_recv()
        ag_y(n).start()
    for n in range(nt):
        ag_y(n).wait_recv()
        ag_c(n).start()
    squares = jnp.zeros((tokens, 1), jnp.float32)
    for n in range(nt):
        ag_c(n).wait_recv()
        wide = ag[n].astype(jnp.float32).reshape(nr, 2, TOK, tn)
        for side in range(2):
            x = wide[:, side].reshape(tokens, tn)
            squares = squares + jnp.sum(x * x, axis=1, keepdims=True)
            lanes = slice(side * w2 + n * tn, side * w2 + (n + 1) * tn)
            lhs[:, lanes] = (x * gain_ref[lanes].reshape(1, tn)).astype(jnp.bfloat16)
    sq_out[...] = jnp.broadcast_to(squares, sq_out.shape)

    def share(p):
        return pl.ds(pl.multiple_of(p * part, 16), part)

    def sq_copy(k):
        p = lax.rem(b + k, nb)
        return remote(
            sq_out.at[share(p)], sq_in.at[k - 1], sq_s.at[k - 1], sq_r.at[k - 1], {"blk": p}
        )

    def gu_copy(j, k):
        p = lax.rem(b + k, nb)
        return remote(
            gu16.at[j, :, share(p)], gu_in.at[j, k - 1],
            gu_s.at[j, k - 1], gu_r.at[j, k - 1], {"blk": p},
        )

    def hid_copy(j, k):
        p = lax.rem(b + k, nb)
        piece = hid.at[j, share(b)]
        return remote(piece, piece, hd_s.at[j, k - 1], hd_r.at[j, k - 1], {"blk": p})

    for k in range(1, nb):
        sq_copy(k).start()
    for copy in weight_copies(0) + weight_copies(1):
        copy.wait()

    def project(j, carry):
        cols = pl.ds(pl.multiple_of(j * fc, fc), fc) if nc > 1 else slice(None)
        for i, w in enumerate((wg, wu)):
            value = jnp.dot(lhs[...], w[:, cols], preferred_element_type=jnp.float32)
            gu32[j, i] = value
            gu16[j, i] = value.astype(jnp.bfloat16)
        for k in range(1, nb):
            gu_copy(j, k).start()
        return carry

    lax.fori_loop(0, nc, project, 0)

    total = sq_out[share(b), 0:1]
    for k in range(1, nb):
        sq_copy(k).wait_recv()
        total = total + sq_in[k - 1, :, 0:1]
    factor = lax.rsqrt(total / (width * nb) + epsilon)

    def activate(j, carry):
        gate = gu32[j, 0, share(b), :]
        up = gu32[j, 1, share(b), :]
        for k in range(1, nb):
            gu_copy(j, k).wait_recv()
            gate = gate + gu_in[j, k - 1, 0].astype(jnp.float32)
            up = up + gu_in[j, k - 1, 1].astype(jnp.float32)
        gate = gate * factor
        up = up * factor
        hid[j, share(b), :] = (gate / (1.0 + jnp.exp(-gate)) * up).astype(jnp.bfloat16)
        for k in range(1, nb):
            hid_copy(j, k).start()
        return carry

    lax.fori_loop(0, nc, activate, 0)
    for copy in weight_copies(2):
        copy.wait()

    def rs_c_copy(n):
        return remote(
            rs.at[n, slots((1 - c) * 2 * zs, 2 * zs)], rs_core.at[n],
            rc_s.at[n], rc_r.at[n], row_of(z, y, 1 - c),
        )

    def rs_y_copy(n):
        return remote(
            rs.at[n, slots((c * 2 + 1 - y) * zs, zs)], rs_y.at[n],
            ry_s.at[n], ry_r.at[n], row_of(z, 1 - y, c),
        )

    def rs_z_copy(n, k):
        zp = lax.rem(z + k, zs)
        return remote(
            rs.at[n, slots(column + zp, 1)], rs_z.at[n, k - 1],
            rz_s.at[n, k - 1], rz_r.at[n, k - 1], row_of(zp, y, c),
        )

    def down(n, j):
        rows = pl.ds(pl.multiple_of(j * fc, fc), fc) if nc > 1 else slice(None)
        sides = []
        for side in range(2):
            cols = pl.ds(pl.multiple_of(side * w2 + n * tn, tn), tn)
            value = jnp.dot(hid[j], wd[rows, cols], preferred_element_type=jnp.float32)
            sides.append(value.reshape(nr, TOK, tn))
        return jnp.concatenate(sides, axis=1).reshape(nr * 16, tn)

    @pl.loop(0, nc - 1)
    def _(j):
        for k in range(1, nb):
            hid_copy(j, k).wait_recv()

        @pl.loop(0, nt)
        def _(n):
            acc[n] = acc[n] + down(n, j)

    for k in range(1, nb):
        hid_copy(nc - 1, k).wait_recv()

    @pl.loop(0, nt)
    def _(n):
        value = acc[n] + down(n, nc - 1)
        acc[n] = value
        rs[n] = value.astype(jnp.bfloat16)
        rs_c_copy(n).start()

    for n in range(nt):
        rs_c_copy(n).wait_recv()
        mine = slots(c * 2 * zs, 2 * zs)
        value = acc[n, mine, :] + rs_core[n].astype(jnp.float32)
        acc[n, mine, :] = value
        rs[n, mine, :] = value.astype(jnp.bfloat16)
        rs_y_copy(n).start()
    for n in range(nt):
        rs_y_copy(n).wait_recv()
        mine = slots(column, zs)
        value = acc[n, mine, :] + rs_y[n].astype(jnp.float32)
        acc[n, mine, :] = value
        rs[n, mine, :] = value.astype(jnp.bfloat16)
        for k in range(1, zs):
            rs_z_copy(n, k).start()
    for n in range(nt):
        value = acc[n, slots(column + z, 1), :]
        for k in range(1, zs):
            rs_z_copy(n, k).wait_recv()
            value = value + rs_z[n, k - 1].astype(jnp.float32)
        for side in range(2):
            lanes = slice(side * w2 + n * tn, side * w2 + (n + 1) * tn)
            base = att[:, lanes].astype(jnp.bfloat16).astype(jnp.float32)
            att[:, lanes] = base + value[side * TOK : (side + 1) * TOK]
    for r in range(rows_here):
        layer_out[r] = att[r * steps : (r + 1) * steps, :].astype(jnp.bfloat16)

    pl.loop(0, half)(lambda k: swap_copy(k).wait_send())
    pl.loop(half + 1, nr)(lambda k: swap_copy(k).wait_send())

    for k in range(1, nb):
        sq_copy(k).wait_send()

    @pl.loop(0, nc)
    def _(j):
        for k in range(1, nb):
            gu_copy(j, k).wait_send()
            hid_copy(j, k).wait_send()

    for n in range(nt):
        for k in range(1, zs):
            ag_z(n, k).wait_send()
            rs_z_copy(n, k).wait_send()
        ag_y(n).wait_send()
        ag_c(n).wait_send()
        rs_c_copy(n).wait_send()
        rs_y_copy(n).wait_send()


def on_device(
    queries,
    new_entries,
    resident,
    swap_area,
    swap_dest,
    page_table,
    lengths,
    norm_gain,
    gate_weight,
    up_weight,
    down_weight,
):
    nr, nb = lax.axis_size("rows"), lax.axis_size("blk")
    rows_here, steps, width = queries.shape
    kvw = new_entries.shape[-1]
    hidden = gate_weight.shape[1]
    res_pages = resident.shape[0]
    pages_row = page_table.shape[1]
    zs = nr // 4
    w2 = width // 2
    tn = min(512, w2)
    nt = w2 // tn
    fc = 256 if hidden % 256 == 0 else hidden
    nc = hidden // fc
    tokens = nr * TOK
    part = tokens // nb
    parts = 4

    index = jnp.arange(swap_dest.shape[0], dtype=jnp.int32)
    same = (swap_dest[:, None] == swap_dest[None, :]) & (index[None, :] < index[:, None])
    slot = swap_dest * CAP + jnp.sum(same.astype(jnp.int32), axis=1)
    goes = slot[None, :] == jnp.arange(nr * CAP, dtype=jnp.int32)[:, None]
    source = jnp.sum(jnp.where(goes, index[None, :], 0), axis=1)

    total_pages = res_pages + nr * CAP
    place = jnp.arange(total_pages * PAGE, dtype=jnp.int32)
    position = jnp.arange(pages_row, dtype=jnp.int32)[:, None] * PAGE + (place % PAGE)[None, :]
    seen = jnp.any(
        (page_table[:, :, None] == (place // PAGE)[None, None, :])
        & (position[None] < lengths[:, None, None]),
        axis=1,
    ).astype(jnp.float32)
    bf, f32 = jnp.bfloat16, jnp.float32
    dma = pltpu.SemaphoreType.DMA
    vm = pl.BlockSpec(memory_space=pltpu.VMEM)
    hbm = pl.BlockSpec(memory_space=pl.ANY)
    peers = max(nb - 1, 1)
    zp = max(zs - 1, 1)
    pair = lambda *shape: [dma(shape), dma(shape)]
    attended, layer = pl.pallas_call(
        functools.partial(layer_kernel, (nr, nb, steps, width, parts, fc)),
        out_shape=[jax.ShapeDtypeStruct(queries.shape, bf)] * 2,
        in_specs=[pl.BlockSpec(memory_space=pltpu.SMEM)] + [vm] * 4 + [hbm] * 5,
        out_specs=[vm] * 2,
        scratch_shapes=[
            pltpu.VMEM(resident.shape, bf),
            pltpu.VMEM(swap_area.shape, bf),
            pltpu.VMEM((nr, CAP, 2, PAGE, kvw), bf),
            pltpu.VMEM((nr, CAP, 2, PAGE, kvw), bf),
            pltpu.VMEM(gate_weight.shape, bf),
            pltpu.VMEM(up_weight.shape, bf),
            pltpu.VMEM(down_weight.shape, bf),
            pltpu.VMEM((TOK, width), f32),
            pltpu.VMEM((nt, nr * 16, tn), bf),
            pltpu.VMEM((tokens, width), bf),
            pltpu.VMEM((nc, 2, tokens, fc), f32),
            pltpu.VMEM((nc, 2, tokens, fc), bf),
            pltpu.VMEM((nc, peers, 2, part, fc), bf),
            pltpu.VMEM((tokens, 128), f32),
            pltpu.VMEM((peers, part, 128), f32),
            pltpu.VMEM((nc, tokens, fc), bf),
            pltpu.VMEM((nt, nr * 16, tn), f32),
            pltpu.VMEM((nt, nr * 16, tn), bf),
            pltpu.VMEM((nt, 2 * zs * 16, tn), bf),
            pltpu.VMEM((nt, zs * 16, tn), bf),
            pltpu.VMEM((nt, zp, 16, tn), bf),
            dma,
            dma((3 * parts,)),
            dma,
        ]
        + pair(nr) + pair(nt, zs) + pair(nt) + pair(nt)
        + pair(nc, peers) + pair(peers) + pair(nc, peers)
        + pair(nt) + pair(nt) + pair(nt, zp),
        compiler_params=pltpu.CompilerParams(
            collective_id=0, has_side_effects=True, vmem_limit_bytes=62 * 1024 * 1024
        ),
        cost_estimate=pl.CostEstimate(
            flops=6 * tokens * width * hidden,
            bytes_accessed=6 * width * hidden,
            transcendentals=tokens * hidden,
        ),
    )(
        source, queries, new_entries, seen, norm_gain.astype(f32),
        resident, swap_area, gate_weight, up_weight, down_weight,
    )
    return attended, layer


def solution(mesh):
    placed = (
        P("rows", None, "blk"),
        P("rows", None, None, "blk"),
        P("rows", None, None, "blk"),
        P("rows", None, None, "blk"),
        P("rows"),
        P("rows", None),
        P("rows"),
        P("blk"),
        P("blk", "rows"),
        P("blk", "rows"),
        P("rows", "blk"),
    )
    return jax.shard_map(
        on_device,
        mesh=mesh,
        in_specs=placed,
        out_specs=(P("rows", None, "blk"), P("rows", None, "blk")),
        check_vma=False,
    )
```
